256 devices in a mesh: ctx: 64 (over x, z_lo, y), dp: 4 (over z_hi, core).
Axes of the slice: x: 4, y: 4, z: 8 (z_hi: 2, z_lo: 4; z = z_hi * 4 + z_lo), core: 2. Of those that a mesh axis runs over, the one named last changes fastest.
Arguments:
- query_in: bfloat16 [256, 131072], P('dp', 'ctx'), may hold values from -6 to 6
- key_in: bfloat16 [256, 131072], P('dp', 'ctx'), may hold values from -6 to 6
- value_in: bfloat16 [256, 131072], P('dp', 'ctx'), may hold values from -6 to 6
- grad_out: bfloat16 [256, 131072], P('dp', 'ctx'), may hold values from -6 to 6
- filter_raw: float32 [64, 131072], P('ctx'), may hold values from -6 to 6
Outputs:
- grad_query: bfloat16 [256, 131072], P('dp', 'ctx')
- grad_key: bfloat16 [256, 131072], P('dp', 'ctx')
- grad_value: bfloat16 [256, 131072], P('dp', 'ctx')
- grad_filter: float32 [64, 131072], P('ctx')
The draws below stay inside these ranges and needn't reach their ends.
All inputs are finite; a program needn't handle non-finite values.
Results may differ from the reference program's by a relative error of at most 0.015.
Values may be sent and summed in bfloat16 or wider, within the bound.
A program may use at most 128 MiB of HBM per device.

```python
import jax
import jax.numpy as jnp
from jax import lax

C = 256
FILT = 64
SEQ = 131072


def shard_levels(key, shape, shards, low, largest):
    level, own = 1.0, jax.random.fold_in(key, 6)
    for position, blocks in shards:
        heights = jnp.exp(jax.random.uniform(jax.random.fold_in(own, position), (blocks,), jnp.float32, low / len(shards), largest / len(shards)))
        level = level * jnp.repeat(heights, shape[position] // blocks).reshape([-1 if axis == position else 1 for axis in range(len(shape))])
    return level


def scatter_about(key, shape, scale, limit, pieces=(), dtype=jnp.bfloat16):
    gain = shard_levels(key, shape, pieces, -0.22, 0.18) if pieces else 1.0
    array = jax.random.normal(key, shape, jnp.float32) * scale * gain
    return jnp.minimum(jnp.maximum(array, -limit), limit).astype(dtype)


def setup_inputs(seed: int = 0) -> dict:
    splits = jax.random.split(jax.random.key(seed), 6)
    return {
        "query_in": scatter_about(splits[0], (C, SEQ), 1.0, 6.0, ((0, 4), (1, 64))),
        "key_in": scatter_about(splits[1], (C, SEQ), 1.0, 6.0, ((0, 4), (1, 64))),
        "value_in": scatter_about(splits[2], (C, SEQ), 1.0, 6.0, ((0, 4), (1, 64))),
        "grad_out": scatter_about(splits[3], (C, SEQ), 1.0, 6.0, ((0, 4), (1, 64))),
        "filter_raw": scatter_about(splits[4], (FILT, SEQ), 1.0, 6.0, ((0, 64),), jnp.float32),
    }


def reference(query_in, key_in, value_in, grad_out, filter_raw):
    length_all = 2 * SEQ
    root = jnp.sqrt(jnp.float32(SEQ))
    filt = filter_raw / root
    gated = (key_in.astype(jnp.float32) * value_in.astype(jnp.float32)).astype(jnp.bfloat16)
    grad_conv = (grad_out.astype(jnp.float32) * query_in.astype(jnp.float32)).astype(jnp.bfloat16)
    spec_filter = jnp.fft.rfft(filt, length_all, axis=1)

    def group_terms(pair):
        gated_block, grad_block = pair
        spec_gated = jnp.fft.rfft(gated_block.astype(jnp.float32), length_all, axis=1)
        spec_grad = jnp.fft.rfft(grad_block.astype(jnp.float32), length_all, axis=1)
        convolved = jnp.fft.irfft(spec_filter * spec_gated, length_all, axis=1)[:, :SEQ]
        grad_mixed = jnp.fft.irfft(jnp.conj(spec_filter) * spec_grad, length_all, axis=1)[:, :SEQ]
        lagged = jnp.fft.irfft(jnp.conj(spec_gated) * spec_grad, length_all, axis=1)[:, :SEQ]
        return (convolved.astype(jnp.bfloat16), grad_mixed.astype(jnp.bfloat16), lagged)
    groups = C // FILT
    convolved, grad_mixed, lagged = lax.map(group_terms, (gated.reshape(groups, FILT, SEQ), grad_conv.reshape(groups, FILT, SEQ)))
    convolved = lax.optimization_barrier(convolved.reshape(C, SEQ)).astype(jnp.float32)
    grad_mixed = lax.optimization_barrier(grad_mixed.reshape(C, SEQ)).astype(jnp.float32)
    grad_query = (grad_out.astype(jnp.float32) * convolved).astype(jnp.bfloat16)
    grad_key = (grad_mixed * value_in.astype(jnp.float32)).astype(jnp.bfloat16)
    grad_value = (grad_mixed * key_in.astype(jnp.float32)).astype(jnp.bfloat16)
    grad_filter = (lax.optimization_barrier(jnp.sum(lagged, axis=0)) / root).astype(jnp.float32)
    return (grad_query, grad_key, grad_value, grad_filter)
```

```python
import functools
import math

import jax
import jax.numpy as jnp
import numpy as np
from jax import lax
from jax.experimental import pallas as pl
from jax.experimental.pallas import tpu as pltpu
from jax.sharding import PartitionSpec as P

LANES = 128
ACROSS = 256
PIECE = 2048
ROWS = PIECE // ACROSS

f32 = jnp.float32
bf16 = jnp.bfloat16


def make_tables(half_rows):
    total = 2 * half_rows * ACROSS
    freq = np.arange(half_rows)[:, None]
    row = np.arange(half_rows)[None, :]
    across = np.arange(ACROSS)
    angle = (row * (2 * freq + 1)) % (4 * half_rows) * (2 * math.pi / (4 * half_rows))
    chunk = half_rows // 2
    cos, sin = np.cos(angle), np.sin(angle)
    first = np.concatenate([cos[:chunk], -sin[:chunk], cos[chunk:], -sin[chunk:]], 0)
    last = np.concatenate([cos, -sin], 0).T
    twist = across[None, :] * (2 * freq + 1) * (2 * math.pi / (2 * total))
    inner = (across[:, None] * across[None, :]) % ACROSS * (2 * math.pi / ACROSS)
    re, im = np.cos(inner), -np.sin(inner)
    second = np.block([[re, im], [-im, re]])
    back = np.block([[re, -im], [im, re]])
    narrow = [t.astype(np.float32).astype(bf16) for t in (first, last, second, back)]
    return narrow + [np.cos(twist).astype(np.float32), -np.sin(twist).astype(np.float32)]


def kernel(
    parts,
    q_ref, k_ref, v_ref, go_ref, h_ref,
    first_hbm, last_hbm, second_hbm, back_hbm, tre_hbm, tim_hbm,
    gq_ref, gk_ref, gv_ref, gf_ref,
    first_ref, last_ref, second_ref, back_ref, tre_ref, tim_ref,
    turn_ref, msg_x, msg_g, msg_c, msg_m, got_x, got_g, got_c, got_m,
    signal_ref, mid_ref, spec_h, spec_x, spec_g,
    lag_ref, lag_in, pair_ref, pair_in, total_ref,
    table_sem, send_sem, recv_sem, pair_send, pair_recv,
):
    half_rows = parts * ROWS
    seq = half_rows * ACROSS
    me = lax.axis_index("ctx")
    group = lax.axis_index("dp")
    core = lax.rem(group, 2)
    high = group // 2
    other_core = high * 2 + (1 - core)
    other_high = (1 - high) * 2 + core
    MESH = pl.DeviceIdType.MESH

    barrier = pltpu.get_barrier_semaphore()

    def greet(step, carry):
        pl.semaphore_signal(
            barrier, inc=1, device_id=(lax.rem(me + step, parts), group), device_id_type=MESH
        )
        return carry

    lax.fori_loop(1, parts, greet, 0)
    pl.semaphore_signal(barrier, inc=1, device_id=(me, other_core), device_id_type=MESH)
    pl.semaphore_signal(barrier, inc=1, device_id=(me, other_high), device_id_type=MESH)

    table_copies = [
        pltpu.make_async_copy(src, dst, table_sem.at[i])
        for i, (src, dst) in enumerate(
            (
                (first_hbm, first_ref),
                (tre_hbm, tre_ref),
                (tim_hbm, tim_ref),
                (second_hbm, second_ref),
                (back_hbm, back_ref),
                (last_hbm, last_ref),
            )
        )
    ]
    for copy in table_copies:
        copy.start()

    def gate(a_ref, b_ref, msg_ref):
        for j in range(PIECE // LANES):
            cols = slice(j * LANES, (j + 1) * LANES)
            slot = (j % 2) * ROWS + j // 2
            turn_ref[pl.ds(slot, parts, stride=16), :] = a_ref[:, cols].astype(f32) * b_ref[
                :, cols
            ].astype(f32)
        msg_ref[...] = turn_ref[...].reshape(parts, 16, LANES).astype(bf16)

    def send_all(msg_ref, got_ref, which):
        def send(step, carry):
            to = lax.rem(me + step, parts)
            pltpu.make_async_remote_copy(
                src_ref=msg_ref.at[to],
                dst_ref=got_ref.at[me],
                send_sem=send_sem.at[which],
                recv_sem=recv_sem.at[which],
                device_id=(to, group),
                device_id_type=MESH,
            ).start()
            return carry

        lax.fori_loop(1, parts, send, 0)
        got_ref[me] = msg_ref[me]

    def whole(ref, sem):
        return pltpu.make_async_copy(
            ref.at[pl.ds(0, parts - 1)], ref.at[pl.ds(0, parts - 1)], sem
        )

    def unfold(got_ref):
        got = got_ref[...].astype(f32)
        for half in range(2):
            signal_ref[:, half * LANES : (half + 1) * LANES] = (
                got[:, half * ROWS : (half + 1) * ROWS, :].reshape(half_rows, LANES).astype(bf16)
            )

    chunk = half_rows // 2

    def forward(spec_ref):
        def body(c, carry):
            rows = pl.ds(pl.multiple_of(c * chunk, chunk), chunk)
            both = jnp.dot(
                first_ref[pl.ds(pl.multiple_of(c * 2 * chunk, 2 * chunk), 2 * chunk), :],
                signal_ref[...],
                preferred_element_type=f32,
            )
            re, im = both[:chunk], both[chunk:]
            tre, tim = tre_ref[rows, :], tim_ref[rows, :]
            turned = jnp.concatenate([re * tre - im * tim, re * tim + im * tre], 1).astype(bf16)
            spec_ref[rows, :] = jnp.dot(turned, second_ref[...], preferred_element_type=f32)
            return carry

        lax.fori_loop(0, 2, body, 0)

    def inverse_mid(a_spec, b_spec, conj):
        def body(c, carry):
            rows = pl.ds(pl.multiple_of(c * chunk, chunk), chunk)
            a_re, a_im = a_spec[rows, :ACROSS], a_spec[rows, ACROSS:]
            b_re, b_im = b_spec[rows, :ACROSS], b_spec[rows, ACROSS:]
            if conj:
                re, im = a_re * b_re + a_im * b_im, a_re * b_im - a_im * b_re
            else:
                re, im = a_re * b_re - a_im * b_im, a_re * b_im + a_im * b_re
            inner = jnp.dot(
                jnp.concatenate([re, im], 1).astype(bf16), back_ref[...], preferred_element_type=f32
            )
            re, im = inner[:, :ACROSS], inner[:, ACROSS:]
            tre, tim = tre_ref[rows, :], tim_ref[rows, :]
            mid_ref[rows, :] = (re * tre + im * tim).astype(bf16)
            mid_ref[pl.ds(pl.multiple_of(half_rows + c * chunk, chunk), chunk), :] = (
                im * tre - re * tim
            ).astype(bf16)
            return carry

        lax.fori_loop(0, 2, body, 0)

    def inverse_rows(c, scale):
        rows = pl.ds(pl.multiple_of(c * chunk, chunk), chunk)
        return (
            jnp.dot(last_ref[rows, :], mid_ref[...], preferred_element_type=f32) * scale
        )

    def inverse_to_msg(a_spec, b_spec, conj, msg_ref):
        inverse_mid(a_spec, b_spec, conj)

        def body(c, carry):
            out = inverse_rows(c, 1.0 / seq)
            out = jnp.concatenate(
                [
                    out[:, :LANES].reshape(parts // 2, ROWS, LANES),
                    out[:, LANES:].reshape(parts // 2, ROWS, LANES),
                ],
                1,
            )
            msg_ref[pl.ds(c * (parts // 2), parts // 2)] = out.astype(bf16)
            return carry

        lax.fori_loop(0, 2, body, 0)

    gate(k_ref, v_ref, msg_x)
    pl.semaphore_wait(barrier, parts + 1)
    send_all(msg_x, got_x, 0)
    gate(go_ref, q_ref, msg_g)
    send_all(msg_g, got_g, 1)

    root = math.sqrt(seq)
    for half in range(2):
        signal_ref[:, half * LANES : (half + 1) * LANES] = (
            h_ref[pl.ds(half, half_rows, stride=2), :] * (1.0 / root)
        ).astype(bf16)
    for copy in table_copies[:4]:
        copy.wait()
    forward(spec_h)

    whole(got_x, recv_sem.at[0]).wait()
    unfold(got_x)
    forward(spec_x)
    for copy in table_copies[4:]:
        copy.wait()
    inverse_to_msg(spec_h, spec_x, False, msg_c)
    send_all(msg_c, got_c, 2)

    whole(got_g, recv_sem.at[1]).wait()
    unfold(got_g)
    forward(spec_g)

    inverse_mid(spec_x, spec_g, True)

    def lag_body(c, carry):
        lag_ref[c] = inverse_rows(c, 1.0 / (seq * root)).astype(bf16)
        return carry

    lax.fori_loop(0, 2, lag_body, 0)

    to_core = pltpu.make_async_remote_copy(
        src_ref=lag_ref.at[1 - core],
        dst_ref=lag_in,
        send_sem=pair_send.at[0],
        recv_sem=pair_recv.at[0],
        device_id=(me, other_core),
        device_id_type=MESH,
    )
    to_core.start()

    inverse_to_msg(spec_h, spec_g, True, msg_m)
    to_core.wait_recv()
    pair_ref[...] = (lag_ref[core].astype(f32) + lag_in[...].astype(f32)).astype(bf16)
    to_high = pltpu.make_async_remote_copy(
        src_ref=pair_ref,
        dst_ref=pair_in,
        send_sem=pair_send.at[1],
        recv_sem=pair_recv.at[1],
        device_id=(me, other_high),
        device_id_type=MESH,
    )
    to_high.start()
    send_all(msg_m, got_m, 3)

    whole(got_c, recv_sem.at[2]).wait()
    turn_ref[...] = got_c[...].astype(f32).reshape(parts * 16, LANES)
    for j in range(PIECE // LANES):
        cols = slice(j * LANES, (j + 1) * LANES)
        slot = (j % 2) * ROWS + j // 2
        conv = turn_ref[pl.ds(slot, parts, stride=16), :]
        gq_ref[:, cols] = (go_ref[:, cols].astype(f32) * conv).astype(bf16)

    to_high.wait_recv()
    total_ref[core] = pair_ref[...].astype(f32) + pair_in[...].astype(f32)
    to_core_again = pltpu.make_async_remote_copy(
        src_ref=total_ref.at[core],
        dst_ref=total_ref.at[core],
        send_sem=pair_send.at[2],
        recv_sem=pair_recv.at[2],
        device_id=(me, other_core),
        device_id_type=MESH,
    )
    to_core_again.start()

    whole(got_m, recv_sem.at[3]).wait()
    turn_ref[...] = got_m[...].astype(f32).reshape(parts * 16, LANES)
    for j in range(PIECE // LANES):
        cols = slice(j * LANES, (j + 1) * LANES)
        slot = (j % 2) * ROWS + j // 2
        mixed = turn_ref[pl.ds(slot, parts, stride=16), :]
        gk_ref[:, cols] = (mixed * v_ref[:, cols].astype(f32)).astype(bf16)
        gv_ref[:, cols] = (mixed * k_ref[:, cols].astype(f32)).astype(bf16)

    to_core_again.wait_recv()
    for c in range(2):
        for half in range(2):
            gf_ref[pl.ds(c * half_rows + half, chunk, stride=2), :] = total_ref[
                c, :, half * LANES : (half + 1) * LANES
            ]
    for which, ref in enumerate((msg_x, msg_g, msg_c, msg_m)):
        whole(ref, send_sem.at[which]).wait()
    to_core.wait_send()
    to_high.wait_send()
    to_core_again.wait_send()


def per_device(parts, query_in, key_in, value_in, grad_out, filter_raw):
    half_rows = parts * ROWS
    seq = half_rows * ACROSS
    tables = make_tables(half_rows)
    vmem = pl.BlockSpec(memory_space=pltpu.VMEM)
    anywhere = pl.BlockSpec(memory_space=pl.ANY)
    window = jax.ShapeDtypeStruct((parts, PIECE), bf16)
    message = pltpu.VMEM((parts, 16, LANES), bf16)
    spectrum = pltpu.VMEM((half_rows, 2 * ACROSS), f32)
    half = (half_rows // 2, ACROSS)
    outs = pl.pallas_call(
        functools.partial(kernel, parts),
        out_shape=(window, window, window, jax.ShapeDtypeStruct((seq // LANES, LANES), f32)),
        in_specs=[vmem] * 5 + [anywhere] * 6,
        out_specs=(vmem, vmem, vmem, vmem),
        scratch_shapes=[pltpu.VMEM(t.shape, t.dtype) for t in tables]
        + [pltpu.VMEM((parts * 16, LANES), f32)]
        + [message] * 8
        + [
            pltpu.VMEM((half_rows, ACROSS), bf16),
            pltpu.VMEM((2 * half_rows, ACROSS), bf16),
            spectrum,
            spectrum,
            spectrum,
            pltpu.VMEM((2,) + half, bf16),
            pltpu.VMEM(half, bf16),
            pltpu.VMEM(half, bf16),
            pltpu.VMEM(half, bf16),
            pltpu.VMEM((2,) + half, f32),
            pltpu.SemaphoreType.DMA((6,)),
            pltpu.SemaphoreType.DMA((4,)),
            pltpu.SemaphoreType.DMA((4,)),
            pltpu.SemaphoreType.DMA((3,)),
            pltpu.SemaphoreType.DMA((3,)),
        ],
        compiler_params=pltpu.CompilerParams(
            collective_id=0, has_side_effects=True, vmem_limit_bytes=48 * 1024 * 1024
        ),
        name="gated_conv_backward",
    )(
        query_in,
        key_in,
        value_in,
        grad_out,
        filter_raw.reshape(seq // LANES, LANES),
        *(jnp.asarray(t) for t in tables),
    )
    return (outs[0], outs[1], outs[2], outs[3].reshape(1, seq))


def solution(mesh):
    return jax.shard_map(
        functools.partial(per_device, mesh.shape["ctx"]),
        mesh=mesh,
        in_specs=(P("dp", "ctx"), P("dp", "ctx"), P("dp", "ctx"), P("dp", "ctx"), P("ctx", None)),
        out_specs=(P("dp", "ctx"), P("dp", "ctx"), P("dp", "ctx"), P("ctx", None)),
        check_vma=False,
    )
```

```python
import functools
import math

import jax
import jax.numpy as jnp
import numpy as np
from jax import lax
from jax.experimental import pallas as pl
from jax.experimental.pallas import tpu as pltpu
from jax.sharding import PartitionSpec as P

LANES = 128
ACROSS = 256
PIECE = 2048
ORDER = (2, 1, 3, 0)
GROUPS = 4
ROWS = PIECE // ACROSS
SLICES = 4
VMEM_GRANT = 52 * 1024 * 1024 + 512 * 1024

f32 = jnp.float32
bf16 = jnp.bfloat16


def make_tables(half_rows):
    total = 2 * half_rows * ACROSS
    freq = np.arange(half_rows)[:, None]
    row = np.arange(half_rows)[None, :]
    across = np.arange(ACROSS)
    angle = (row * (2 * freq + 1)) % (4 * half_rows) * (2 * math.pi / (4 * half_rows))
    chunk = half_rows // 2
    cos, sin = np.cos(angle), np.sin(angle)
    first = np.concatenate([cos[:chunk], -sin[:chunk], cos[chunk:], -sin[chunk:]], 0)
    last = np.concatenate([cos, -sin], 0).T
    twist = across[None, :] * (2 * freq + 1) * (2 * math.pi / (2 * total))
    inner = (across[:, None] * across[None, :]) % ACROSS * (2 * math.pi / ACROSS)
    re, im = np.cos(inner), -np.sin(inner)
    second = np.block([[re, im], [-im, re]])
    back = np.block([[re, -im], [im, re]])
    narrow = [t.astype(np.float32).astype(bf16) for t in (first, last, second, back)]
    return narrow + [np.cos(twist).astype(np.float32), -np.sin(twist).astype(np.float32)]


def kernel(
    parts,
    q_hbm, k_hbm, v_hbm, go_hbm, h_hbm,
    first_hbm, last_hbm, second_hbm, back_hbm, tre_hbm, tim_hbm,
    gq_ref, gk_ref, gv_ref, gf0_ref, gf1_ref,
    q_ref, k_ref, v_ref, go_ref, h_ref,
    first_ref, last_ref, second_ref, back_ref, tre_ref, tim_ref,
    turn_ref, msg_x, msg_g, msg_c, msg_m, got_x, got_g, got_c, got_m,
    signal_ref, mid_ref, spec_h, spec_x, spec_g,
    lag_ref, lag_in, pair_ref, pair_in, total_ref,
    window_sem, load_sem, send_sem, recv_sem, pair_send, pair_recv,
):
    half_rows = parts * ROWS
    seq = half_rows * ACROSS
    me = lax.axis_index("ctx")
    group = lax.axis_index("dp")
    core = lax.rem(group, 2)
    high = group // 2
    other_core = high * 2 + (1 - core)
    other_high = (1 - high) * 2 + core
    MESH = pl.DeviceIdType.MESH

    size = parts // GROUPS
    plane, spot = me // size, lax.rem(me, size)

    def sent_rows(i):
        return pl.multiple_of(lax.rem(plane + ORDER[i], GROUPS) * size, size)

    def got_rows(i):
        return pl.multiple_of(lax.rem(plane + GROUPS - ORDER[i], GROUPS) * size, size)

    barrier = pltpu.get_barrier_semaphore()

    def greet(step, carry):
        pl.semaphore_signal(
            barrier, inc=1, device_id=(lax.rem(me + step, parts), group), device_id_type=MESH
        )
        return carry

    lax.fori_loop(1, parts, greet, 0)
    pl.semaphore_signal(barrier, inc=1, device_id=(me, other_core), device_id_type=MESH)
    pl.semaphore_signal(barrier, inc=1, device_id=(me, other_high), device_id_type=MESH)

    windows = ((k_hbm, k_ref), (v_hbm, v_ref), (go_hbm, go_ref), (q_hbm, q_ref))
    window_loads = []
    for pair in (windows[:2], windows[2:]):
        for i in range(GROUPS):
            for src, dst in pair:
                rows = pl.ds(sent_rows(i), size)
                load = pltpu.make_async_copy(
                    src.at[rows], dst.at[rows], window_sem.at[len(window_loads)]
                )
                load.start()
                window_loads.append(load)
    loads = [
        pltpu.make_async_copy(src, dst, load_sem.at[i])
        for i, (src, dst) in enumerate(
            (
                (h_hbm, h_ref),
                (first_hbm, first_ref),
                (tre_hbm, tre_ref),
                (tim_hbm, tim_ref),
                (second_hbm, second_ref),
                (back_hbm, back_ref),
                (last_hbm, last_ref),
            )
        )
    ]
    for load in loads:
        load.start()

    def gate(a_ref, b_ref, msg_ref, i):
        start = sent_rows(i)
        rows = pl.ds(start, size)
        for j in range(PIECE // LANES):
            cols = slice(j * LANES, (j + 1) * LANES)
            slot = (j % 2) * ROWS + j // 2
            turn_ref[pl.ds(slot, size, stride=16), :] = a_ref[rows, cols].astype(f32) * b_ref[
                rows, cols
            ].astype(f32)
        msg_ref[rows] = turn_ref[...].reshape(size, 16, LANES).astype(bf16)

    def send_group(msg_ref, got_ref, which, i):
        start = sent_rows(i)

        def send(step, carry):
            to = start + lax.rem(spot + step, size)
            pltpu.make_async_remote_copy(
                src_ref=msg_ref.at[to],
                dst_ref=got_ref.at[me],
                send_sem=send_sem.at[which],
                recv_sem=recv_sem.at[which, i],
                device_id=(to, group),
                device_id_type=MESH,
            ).start()
            return carry

        lax.fori_loop(1 if ORDER[i] == 0 else 0, size, send, 0)
        if ORDER[i] == 0:
            got_ref[me] = msg_ref[me]

    def wait_group(got_ref, which, i):
        count = size - 1 if ORDER[i] == 0 else size
        if count:
            some = got_ref.at[pl.ds(0, count)]
            pltpu.make_async_copy(some, some, recv_sem.at[which, i]).wait()

    def wait_all(got_ref, which):
        for i in range(GROUPS):
            wait_group(got_ref, which, i)

    def unfold(got_ref):
        got = got_ref[...].astype(f32)
        for half in range(2):
            signal_ref[:, half * LANES : (half + 1) * LANES] = (
                got[:, half * ROWS : (half + 1) * ROWS, :].reshape(half_rows, LANES).astype(bf16)
            )

    chunk = half_rows // 2

    def forward(spec_ref):
        def body(c, carry):
            rows = pl.ds(pl.multiple_of(c * chunk, chunk), chunk)
            both = jnp.dot(
                first_ref[pl.ds(pl.multiple_of(c * 2 * chunk, 2 * chunk), 2 * chunk), :],
                signal_ref[...],
                preferred_element_type=f32,
            )
            re, im = both[:chunk], both[chunk:]
            tre, tim = tre_ref[rows, :], tim_ref[rows, :]
            turned = jnp.concatenate([re * tre - im * tim, re * tim + im * tre], 1).astype(bf16)
            spec_ref[rows, :] = jnp.dot(turned, second_ref[...], preferred_element_type=f32)
            return carry

        lax.fori_loop(0, 2, body, 0)

    def inverse_mid(a_spec, b_spec, conj):
        def body(c, carry):
            rows = pl.ds(pl.multiple_of(c * chunk, chunk), chunk)
            a_re, a_im = a_spec[rows, :ACROSS], a_spec[rows, ACROSS:]
            b_re, b_im = b_spec[rows, :ACROSS], b_spec[rows, ACROSS:]
            if conj:
                re, im = a_re * b_re + a_im * b_im, a_re * b_im - a_im * b_re
            else:
                re, im = a_re * b_re - a_im * b_im, a_re * b_im + a_im * b_re
            inner = jnp.dot(
                jnp.concatenate([re, im], 1).astype(bf16), back_ref[...], preferred_element_type=f32
            )
            re, im = inner[:, :ACROSS], inner[:, ACROSS:]
            tre, tim = tre_ref[rows, :], tim_ref[rows, :]
            mid_ref[rows, :] = (re * tre + im * tim).astype(bf16)
            mid_ref[pl.ds(pl.multiple_of(half_rows + c * chunk, chunk), chunk), :] = (
                im * tre - re * tim
            ).astype(bf16)
            return carry

        lax.fori_loop(0, 2, body, 0)

    def inverse_rows_and_send(msg_ref, got_ref, which):
        for i in range(GROUPS):
            start = sent_rows(i)
            rows = pl.ds(pl.multiple_of(start * ROWS, size * ROWS), size * ROWS)
            out = jnp.dot(last_ref[rows, :], mid_ref[...], preferred_element_type=f32) * (1.0 / seq)
            out = jnp.concatenate(
                [
                    out[:, :LANES].reshape(size, ROWS, LANES),
                    out[:, LANES:].reshape(size, ROWS, LANES),
                ],
                1,
            )
            msg_ref[pl.ds(start, size)] = out.astype(bf16)
            send_group(msg_ref, got_ref, which, i)

    for i in range(GROUPS):
        window_loads[2 * i].wait()
        window_loads[2 * i + 1].wait()
        gate(k_ref, v_ref, msg_x, i)
        if i == 0:
            pl.semaphore_wait(barrier, parts + 1)
        send_group(msg_x, got_x, 0, i)
    for i in range(GROUPS):
        window_loads[2 * (GROUPS + i)].wait()
        window_loads[2 * (GROUPS + i) + 1].wait()
        gate(go_ref, q_ref, msg_g, i)
        send_group(msg_g, got_g, 1, i)

    root = math.sqrt(seq)
    loads[0].wait()
    for half in range(2):
        signal_ref[:, half * LANES : (half + 1) * LANES] = (
            h_ref[pl.ds(half, half_rows, stride=2), :] * (1.0 / root)
        ).astype(bf16)
    for load in loads[1:5]:
        load.wait()
    forward(spec_h)

    wait_all(got_x, 0)
    unfold(got_x)
    forward(spec_x)
    for load in loads[5:]:
        load.wait()
    inverse_mid(spec_h, spec_x, False)
    inverse_rows_and_send(msg_c, got_c, 2)

    wait_all(got_g, 1)
    unfold(got_g)
    forward(spec_g)

    inverse_mid(spec_x, spec_g, True)

    def lag_body(c, carry):
        rows = pl.ds(pl.multiple_of(c * chunk, chunk), chunk)
        lag_ref[c] = (
            jnp.dot(last_ref[rows, :], mid_ref[...], preferred_element_type=f32)
            * (1.0 / (seq * root))
        ).astype(bf16)
        return carry

    lax.fori_loop(0, 2, lag_body, 0)

    to_core = pltpu.make_async_remote_copy(
        src_ref=lag_ref.at[1 - core],
        dst_ref=lag_in,
        send_sem=pair_send.at[0],
        recv_sem=pair_recv.at[0],
        device_id=(me, other_core),
        device_id_type=MESH,
    )
    to_core.start()

    inverse_mid(spec_h, spec_g, True)
    to_core.wait_recv()
    pair_ref[...] = (lag_ref[core].astype(f32) + lag_in[...].astype(f32)).astype(bf16)
    to_high = pltpu.make_async_remote_copy(
        src_ref=pair_ref,
        dst_ref=pair_in,
        send_sem=pair_send.at[1],
        recv_sem=pair_recv.at[1],
        device_id=(me, other_high),
        device_id_type=MESH,
    )
    to_high.start()
    inverse_rows_and_send(msg_m, got_m, 3)

    def finish(got_ref, which, i, terms):
        wait_group(got_ref, which, i)
        rows = pl.ds(got_rows(i), size)
        turn_ref[...] = got_ref[rows].astype(f32).reshape(size * 16, LANES)
        for j in range(PIECE // LANES):
            cols = slice(j * LANES, (j + 1) * LANES)
            slot = (j % 2) * ROWS + j // 2
            value = turn_ref[pl.ds(slot, size, stride=16), :]
            for factor_ref, out_ref in terms:
                out_ref[rows, cols] = (factor_ref[rows, cols].astype(f32) * value).astype(bf16)

    for i in range(GROUPS):
        finish(got_c, 2, i, ((go_ref, gq_ref),))

    to_high.wait_recv()
    total_ref[core] = pair_ref[...].astype(f32) + pair_in[...].astype(f32)
    to_core_again = pltpu.make_async_remote_copy(
        src_ref=total_ref.at[core],
        dst_ref=total_ref.at[core],
        send_sem=pair_send.at[2],
        recv_sem=pair_recv.at[2],
        device_id=(me, other_core),
        device_id_type=MESH,
    )
    to_core_again.start()

    to_core_again.wait_recv()
    for c, gf_ref in enumerate((gf0_ref, gf1_ref)):
        for half in range(2):
            gf_ref[pl.ds(half, chunk, stride=2), :] = total_ref[
                c, :, half * LANES : (half + 1) * LANES
            ]

    for i in range(GROUPS):
        finish(got_m, 3, i, ((v_ref, gk_ref), (k_ref, gv_ref)))

    for which, ref in enumerate((msg_x, msg_g, msg_c, msg_m)):
        some = ref.at[pl.ds(0, parts - 1)]
        pltpu.make_async_copy(some, some, send_sem.at[which]).wait()
    to_core.wait_send()
    to_high.wait_send()
    to_core_again.wait_send()


def write_out(*refs):
    sources, targets, sem = refs[:5], refs[5:9], refs[9]
    copies = []
    for i, source in enumerate(sources):
        height = source.shape[0]
        step = height // SLICES
        target, base = (targets[i], 0) if i < 3 else (targets[3], (i - 3) * height)
        for part in range(SLICES):
            copies.append(
                pltpu.make_async_copy(
                    source.at[pl.ds(part * step, step)],
                    target.at[pl.ds(base + part * step, step)],
                    sem.at[len(copies)],
                )
            )
    for copy in copies:
        copy.start()
    for copy in copies:
        copy.wait()


def per_device(parts, query_in, key_in, value_in, grad_out, filter_raw):
    half_rows = parts * ROWS
    seq = half_rows * ACROSS
    tables = make_tables(half_rows)
    vmem = pl.BlockSpec(memory_space=pltpu.VMEM)
    hbm = pl.BlockSpec(memory_space=pltpu.HBM)
    window = jax.ShapeDtypeStruct((parts, PIECE), bf16)
    taps = jax.ShapeDtypeStruct((seq // (2 * LANES), LANES), f32)
    message = pltpu.VMEM((parts, 16, LANES), bf16)
    spectrum = pltpu.VMEM((half_rows, 2 * ACROSS), f32)
    half = (half_rows // 2, ACROSS)
    outs = pl.pallas_call(
        functools.partial(kernel, parts),
        out_shape=(window, window, window, taps, taps),
        in_specs=[hbm] * 11,
        out_specs=(vmem,) * 5,
        scratch_shapes=[pltpu.VMEM((parts, PIECE), bf16)] * 4
        + [pltpu.VMEM((seq // LANES, LANES), f32)]
        + [pltpu.VMEM(t.shape, t.dtype) for t in tables]
        + [pltpu.VMEM((parts // GROUPS * 16, LANES), f32)]
        + [message] * 8
        + [
            pltpu.VMEM((half_rows, ACROSS), bf16),
            pltpu.VMEM((2 * half_rows, ACROSS), bf16),
            spectrum,
            spectrum,
            spectrum,
            pltpu.VMEM((2,) + half, bf16),
            pltpu.VMEM(half, bf16),
            pltpu.VMEM(half, bf16),
            pltpu.VMEM(half, bf16),
            pltpu.VMEM((2,) + half, f32),
            pltpu.SemaphoreType.DMA((4 * GROUPS,)),
            pltpu.SemaphoreType.DMA((7,)),
            pltpu.SemaphoreType.DMA((4,)),
            pltpu.SemaphoreType.DMA((4, GROUPS)),
            pltpu.SemaphoreType.DMA((3,)),
            pltpu.SemaphoreType.DMA((3,)),
        ],
        compiler_params=pltpu.CompilerParams(
            collective_id=0, has_side_effects=True, vmem_limit_bytes=VMEM_GRANT
        ),
        name="gated_conv_backward",
    )(
        query_in,
        key_in,
        value_in,
        grad_out,
        filter_raw.reshape(seq // LANES, LANES),
        *(jnp.asarray(t) for t in tables),
    )
    outs = pl.pallas_call(
        write_out,
        out_shape=(window, window, window, jax.ShapeDtypeStruct((seq // LANES, LANES), f32)),
        in_specs=[pl.BlockSpec(memory_space=pl.ANY)] * 5,
        out_specs=[hbm] * 4,
        scratch_shapes=[pltpu.SemaphoreType.DMA((5 * SLICES,))],
        compiler_params=pltpu.CompilerParams(vmem_limit_bytes=VMEM_GRANT),
        name="write_out",
    )(*outs)
    return (outs[0], outs[1], outs[2], outs[3].reshape(1, seq))


def solution(mesh):
    return jax.shard_map(
        functools.partial(per_device, mesh.shape["ctx"]),
        mesh=mesh,
        in_specs=(P("dp", "ctx"), P("dp", "ctx"), P("dp", "ctx"), P("dp", "ctx"), P("ctx", None)),
        out_specs=(P("dp", "ctx"), P("dp", "ctx"), P("dp", "ctx"), P("ctx", None)),
        check_vma=False,
    )
```

```python
import functools
import math

import jax
import jax.numpy as jnp
import numpy as np
from jax import lax
from jax.experimental import pallas as pl
from jax.experimental.pallas import tpu as pltpu
from jax.sharding import PartitionSpec as P

LANES = 128
ACROSS = 256
PIECE = 2048
ORDER = (2, 1, 3, 0)
GROUPS = 4
ROWS = PIECE // ACROSS
SLICES = 4
VMEM_GRANT = 52 * 1024 * 1024 + 512 * 1024

f32 = jnp.float32
bf16 = jnp.bfloat16


def make_tables(half_rows):
    total = 2 * half_rows * ACROSS
    freq = np.arange(half_rows)[:, None]
    row = np.arange(half_rows)[None, :]
    across = np.arange(ACROSS)
    angle = (row * (2 * freq + 1)) % (4 * half_rows) * (2 * math.pi / (4 * half_rows))
    chunk = half_rows // 2
    cos, sin = np.cos(angle), np.sin(angle)
    first = np.concatenate([cos[:chunk], -sin[:chunk], cos[chunk:], -sin[chunk:]], 0)
    last = np.concatenate([cos, -sin], 0).T
    twist = across[None, :] * (2 * freq + 1) * (2 * math.pi / (2 * total))
    inner = (across[:, None] * across[None, :]) % ACROSS * (2 * math.pi / ACROSS)
    re, im = np.cos(inner), -np.sin(inner)
    second = np.block([[re, im], [-im, re]])
    back = np.block([[re, -im], [im, re]])
    narrow = [t.astype(np.float32).astype(bf16) for t in (first, last, second, back)]
    return narrow + [np.cos(twist).astype(np.float32), -np.sin(twist).astype(np.float32)]


def kernel(
    parts,
    q_hbm, k_hbm, v_hbm, go_hbm, h_hbm,
    first_hbm, last_hbm, second_hbm, back_hbm, tre_hbm, tim_hbm,
    gq_ref, gk_ref, gv_ref, gf0_ref, gf1_ref,
    q_ref, k_ref, v_ref, go_ref, h_ref,
    first_ref, last_ref, second_ref, back_ref, tre_ref, tim_ref,
    turn_ref, msg_x, msg_g, msg_c, msg_m, got_x, got_g, got_c, got_m,
    signal_ref, mid_ref, spec_h, spec_x, spec_g,
    lag_ref, lag_in, pair_ref, pair_in, total_ref,
    window_sem, load_sem, send_sem, recv_sem, pair_send, pair_recv,
    high_send, high_recv, share_send, share_recv,
):
    half_rows = parts * ROWS
    seq = half_rows * ACROSS
    me = lax.axis_index("ctx")
    group = lax.axis_index("dp")
    core = lax.rem(group, 2)
    high = group // 2
    other_core = high * 2 + (1 - core)
    other_high = (1 - high) * 2 + core
    MESH = pl.DeviceIdType.MESH

    size = parts // GROUPS
    plane, spot = me // size, lax.rem(me, size)

    def sent_rows(i):
        return pl.multiple_of(lax.rem(plane + ORDER[i], GROUPS) * size, size)

    def got_rows(i):
        return pl.multiple_of(lax.rem(plane + GROUPS - ORDER[i], GROUPS) * size, size)

    barrier = pltpu.get_barrier_semaphore()

    def greet(step, carry):
        pl.semaphore_signal(
            barrier, inc=1, device_id=(lax.rem(me + step, parts), group), device_id_type=MESH
        )
        return carry

    lax.fori_loop(1, parts, greet, 0)
    pl.semaphore_signal(barrier, inc=1, device_id=(me, other_core), device_id_type=MESH)
    pl.semaphore_signal(barrier, inc=1, device_id=(me, other_high), device_id_type=MESH)

    windows = ((k_hbm, k_ref), (v_hbm, v_ref), (go_hbm, go_ref), (q_hbm, q_ref))
    window_loads = []
    for pair in (windows[:2], windows[2:]):
        for i in range(GROUPS):
            for src, dst in pair:
                rows = pl.ds(sent_rows(i), size)
                load = pltpu.make_async_copy(
                    src.at[rows], dst.at[rows], window_sem.at[len(window_loads)]
                )
                load.start()
                window_loads.append(load)
    loads = [
        pltpu.make_async_copy(src, dst, load_sem.at[i])
        for i, (src, dst) in enumerate(
            (
                (h_hbm, h_ref),
                (first_hbm, first_ref),
                (tre_hbm, tre_ref),
                (tim_hbm, tim_ref),
                (second_hbm, second_ref),
                (back_hbm, back_ref),
                (last_hbm, last_ref),
            )
        )
    ]
    for load in loads:
        load.start()

    def gate(a_ref, b_ref, msg_ref, i):
        start = sent_rows(i)
        rows = pl.ds(start, size)
        for j in range(PIECE // LANES):
            cols = slice(j * LANES, (j + 1) * LANES)
            slot = (j % 2) * ROWS + j // 2
            turn_ref[pl.ds(slot, size, stride=16), :] = a_ref[rows, cols].astype(f32) * b_ref[
                rows, cols
            ].astype(f32)
        msg_ref[rows] = turn_ref[...].reshape(size, 16, LANES).astype(bf16)

    def send_group(msg_ref, got_ref, which, i):
        start = sent_rows(i)

        def send(step, carry):
            to = start + lax.rem(spot + step, size)
            pltpu.make_async_remote_copy(
                src_ref=msg_ref.at[to],
                dst_ref=got_ref.at[me],
                send_sem=send_sem.at[which],
                recv_sem=recv_sem.at[which, i],
                device_id=(to, group),
                device_id_type=MESH,
            ).start()
            return carry

        lax.fori_loop(1 if ORDER[i] == 0 else 0, size, send, 0)
        if ORDER[i] == 0:
            got_ref[me] = msg_ref[me]

    def wait_group(got_ref, which, i):
        count = size - 1 if ORDER[i] == 0 else size
        if count:
            some = got_ref.at[pl.ds(0, count)]
            pltpu.make_async_copy(some, some, recv_sem.at[which, i]).wait()

    def wait_all(got_ref, which):
        for i in range(GROUPS):
            wait_group(got_ref, which, i)

    def unfold(got_ref):
        got = got_ref[...].astype(f32)
        for half in range(2):
            signal_ref[:, half * LANES : (half + 1) * LANES] = (
                got[:, half * ROWS : (half + 1) * ROWS, :].reshape(half_rows, LANES).astype(bf16)
            )

    chunk = half_rows // 2

    def forward(spec_ref):
        def body(c, carry):
            rows = pl.ds(pl.multiple_of(c * chunk, chunk), chunk)
            both = jnp.dot(
                first_ref[pl.ds(pl.multiple_of(c * 2 * chunk, 2 * chunk), 2 * chunk), :],
                signal_ref[...],
                preferred_element_type=f32,
            )
            re, im = both[:chunk], both[chunk:]
            tre, tim = tre_ref[rows, :], tim_ref[rows, :]
            turned = jnp.concatenate([re * tre - im * tim, re * tim + im * tre], 1).astype(bf16)
            spec_ref[rows, :] = jnp.dot(turned, second_ref[...], preferred_element_type=f32)
            return carry

        lax.fori_loop(0, 2, body, 0)

    def inverse_mid(a_spec, b_spec, conj):
        def body(c, carry):
            rows = pl.ds(pl.multiple_of(c * chunk, chunk), chunk)
            a_re, a_im = a_spec[rows, :ACROSS], a_spec[rows, ACROSS:]
            b_re, b_im = b_spec[rows, :ACROSS], b_spec[rows, ACROSS:]
            if conj:
                re, im = a_re * b_re + a_im * b_im, a_re * b_im - a_im * b_re
            else:
                re, im = a_re * b_re - a_im * b_im, a_re * b_im + a_im * b_re
            inner = jnp.dot(
                jnp.concatenate([re, im], 1).astype(bf16), back_ref[...], preferred_element_type=f32
            )
            re, im = inner[:, :ACROSS], inner[:, ACROSS:]
            tre, tim = tre_ref[rows, :], tim_ref[rows, :]
            mid_ref[rows, :] = (re * tre + im * tim).astype(bf16)
            mid_ref[pl.ds(pl.multiple_of(half_rows + c * chunk, chunk), chunk), :] = (
                im * tre - re * tim
            ).astype(bf16)
            return carry

        lax.fori_loop(0, 2, body, 0)

    def inverse_rows_and_send(msg_ref, got_ref, which):
        for i in range(GROUPS):
            start = sent_rows(i)
            rows = pl.ds(pl.multiple_of(start * ROWS, size * ROWS), size * ROWS)
            out = jnp.dot(last_ref[rows, :], mid_ref[...], preferred_element_type=f32) * (1.0 / seq)
            out = jnp.concatenate(
                [
                    out[:, :LANES].reshape(size, ROWS, LANES),
                    out[:, LANES:].reshape(size, ROWS, LANES),
                ],
                1,
            )
            msg_ref[pl.ds(start, size)] = out.astype(bf16)
            send_group(msg_ref, got_ref, which, i)

    for i in range(GROUPS):
        window_loads[2 * i].wait()
        window_loads[2 * i + 1].wait()
        gate(k_ref, v_ref, msg_x, i)
        if i == 0:
            pl.semaphore_wait(barrier, parts + 1)
        send_group(msg_x, got_x, 0, i)
    for i in range(GROUPS):
        window_loads[2 * (GROUPS + i)].wait()
        window_loads[2 * (GROUPS + i) + 1].wait()
        gate(go_ref, q_ref, msg_g, i)
        send_group(msg_g, got_g, 1, i)

    root = math.sqrt(seq)
    loads[0].wait()
    for half in range(2):
        signal_ref[:, half * LANES : (half + 1) * LANES] = (
            h_ref[pl.ds(half, half_rows, stride=2), :] * (1.0 / root)
        ).astype(bf16)
    for load in loads[1:5]:
        load.wait()
    forward(spec_h)

    wait_all(got_x, 0)
    unfold(got_x)
    forward(spec_x)
    for load in loads[5:]:
        load.wait()
    inverse_mid(spec_h, spec_x, False)
    inverse_rows_and_send(msg_c, got_c, 2)

    wait_all(got_g, 1)
    unfold(got_g)
    forward(spec_g)

    inverse_mid(spec_h, spec_g, True)
    inverse_rows_and_send(msg_m, got_m, 3)
    inverse_mid(spec_x, spec_g, True)

    def lag_body(c, carry):
        rows = pl.ds(pl.multiple_of(c * chunk, chunk), chunk)
        lag_ref[c] = (
            jnp.dot(last_ref[rows, :], mid_ref[...], preferred_element_type=f32)
            * (1.0 / (seq * root))
        ).astype(bf16)
        return carry

    lax.fori_loop(0, 2, lag_body, 0)

    to_core = pltpu.make_async_remote_copy(
        src_ref=lag_ref.at[1 - core],
        dst_ref=lag_in,
        send_sem=pair_send.at[0],
        recv_sem=pair_recv.at[0],
        device_id=(me, other_core),
        device_id_type=MESH,
    )
    to_core.start()

    to_core.wait_recv()
    pair_ref[...] = (lag_ref[core].astype(f32) + lag_in[...].astype(f32)).astype(bf16)
    quarter = half_rows // 8
    to_high = [
        pltpu.make_async_remote_copy(
            src_ref=pair_ref.at[pl.ds(n * quarter, quarter)],
            dst_ref=pair_in.at[pl.ds(n * quarter, quarter)],
            send_sem=high_send.at[n],
            recv_sem=high_recv.at[n],
            device_id=(me, other_high),
            device_id_type=MESH,
        )
        for n in range(4)
    ]
    for copy in to_high:
        copy.start()

    def finish(got_ref, which, i, terms):
        wait_group(got_ref, which, i)
        rows = pl.ds(got_rows(i), size)
        turn_ref[...] = got_ref[rows].astype(f32).reshape(size * 16, LANES)
        for j in range(PIECE // LANES):
            cols = slice(j * LANES, (j + 1) * LANES)
            slot = (j % 2) * ROWS + j // 2
            value = turn_ref[pl.ds(slot, size, stride=16), :]
            for factor_ref, out_ref in terms:
                out_ref[rows, cols] = (factor_ref[rows, cols].astype(f32) * value).astype(bf16)

    for i in range(GROUPS):
        finish(got_c, 2, i, ((go_ref, gq_ref),))

    for i in (0, 1, 2, 3):
        finish(got_m, 3, i, ((v_ref, gk_ref), (k_ref, gv_ref)))

    to_core_again = []
    for n in range(4):
        rows = pl.ds(n * quarter, quarter)
        to_high[n].wait_recv()
        total_ref[core, rows] = pair_ref[rows].astype(f32) + pair_in[rows].astype(f32)
        copy = pltpu.make_async_remote_copy(
            src_ref=total_ref.at[core, rows],
            dst_ref=total_ref.at[core, rows],
            send_sem=share_send.at[n],
            recv_sem=share_recv.at[n],
            device_id=(me, other_core),
            device_id_type=MESH,
        )
        copy.start()
        to_core_again.append(copy)
    for copy in to_core_again:
        copy.wait_recv()
    for c, gf_ref in enumerate((gf0_ref, gf1_ref)):
        for half in range(2):
            gf_ref[pl.ds(half, chunk, stride=2), :] = total_ref[
                c, :, half * LANES : (half + 1) * LANES
            ]

    for which, ref in enumerate((msg_x, msg_g, msg_c, msg_m)):
        some = ref.at[pl.ds(0, parts - 1)]
        pltpu.make_async_copy(some, some, send_sem.at[which]).wait()
    to_core.wait_send()
    for copy in to_high + to_core_again:
        copy.wait_send()


def write_out(*refs):
    sources, targets, sem = refs[:5], refs[5:9], refs[9]
    copies = []
    for i, source in enumerate(sources):
        height = source.shape[0]
        step = height // SLICES
        target, base = (targets[i], 0) if i < 3 else (targets[3], (i - 3) * height)
        for part in range(SLICES):
            copies.append(
                pltpu.make_async_copy(
                    source.at[pl.ds(part * step, step)],
                    target.at[pl.ds(base + part * step, step)],
                    sem.at[len(copies)],
                )
            )
    for copy in copies:
        copy.start()
    for copy in copies:
        copy.wait()


def per_device(parts, query_in, key_in, value_in, grad_out, filter_raw):
    half_rows = parts * ROWS
    seq = half_rows * ACROSS
    tables = make_tables(half_rows)
    vmem = pl.BlockSpec(memory_space=pltpu.VMEM)
    hbm = pl.BlockSpec(memory_space=pltpu.HBM)
    window = jax.ShapeDtypeStruct((parts, PIECE), bf16)
    taps = jax.ShapeDtypeStruct((seq // (2 * LANES), LANES), f32)
    message = pltpu.VMEM((parts, 16, LANES), bf16)
    spectrum = pltpu.VMEM((half_rows, 2 * ACROSS), f32)
    half = (half_rows // 2, ACROSS)
    outs = pl.pallas_call(
        functools.partial(kernel, parts),
        out_shape=(window, window, window, taps, taps),
        in_specs=[hbm] * 11,
        out_specs=(vmem,) * 5,
        scratch_shapes=[pltpu.VMEM((parts, PIECE), bf16)] * 4
        + [pltpu.VMEM((seq // LANES, LANES), f32)]
        + [pltpu.VMEM(t.shape, t.dtype) for t in tables]
        + [pltpu.VMEM((parts // GROUPS * 16, LANES), f32)]
        + [message] * 8
        + [
            pltpu.VMEM((half_rows, ACROSS), bf16),
            pltpu.VMEM((2 * half_rows, ACROSS), bf16),
            spectrum,
            spectrum,
            spectrum,
            pltpu.VMEM((2,) + half, bf16),
            pltpu.VMEM(half, bf16),
            pltpu.VMEM(half, bf16),
            pltpu.VMEM(half, bf16),
            pltpu.VMEM((2,) + half, f32),
            pltpu.SemaphoreType.DMA((4 * GROUPS,)),
            pltpu.SemaphoreType.DMA((7,)),
            pltpu.SemaphoreType.DMA((4,)),
            pltpu.SemaphoreType.DMA((4, GROUPS)),
            pltpu.SemaphoreType.DMA((1,)),
            pltpu.SemaphoreType.DMA((1,)),
            pltpu.SemaphoreType.DMA((4,)),
            pltpu.SemaphoreType.DMA((4,)),
            pltpu.SemaphoreType.DMA((4,)),
            pltpu.SemaphoreType.DMA((4,)),
        ],
        compiler_params=pltpu.CompilerParams(
            collective_id=0, has_side_effects=True, vmem_limit_bytes=VMEM_GRANT
        ),
        name="gated_conv_backward",
    )(
        query_in,
        key_in,
        value_in,
        grad_out,
        filter_raw.reshape(seq // LANES, LANES),
        *(jnp.asarray(t) for t in tables),
    )
    outs = pl.pallas_call(
        write_out,
        out_shape=(window, window, window, jax.ShapeDtypeStruct((seq // LANES, LANES), f32)),
        in_specs=[pl.BlockSpec(memory_space=pl.ANY)] * 5,
        out_specs=[hbm] * 4,
        scratch_shapes=[pltpu.SemaphoreType.DMA((5 * SLICES,))],
        compiler_params=pltpu.CompilerParams(vmem_limit_bytes=VMEM_GRANT),
        name="write_out",
    )(*outs)
    return (outs[0], outs[1], outs[2], outs[3].reshape(1, seq))


def solution(mesh):
    return jax.shard_map(
        functools.partial(per_device, mesh.shape["ctx"]),
        mesh=mesh,
        in_specs=(P("dp", "ctx"), P("dp", "ctx"), P("dp", "ctx"), P("dp", "ctx"), P("ctx", None)),
        out_specs=(P("dp", "ctx"), P("dp", "ctx"), P("dp", "ctx"), P("ctx", None)),
        check_vma=False,
    )
```

```python
import functools
import math

import jax
import jax.numpy as jnp
import numpy as np
from jax import lax
from jax.experimental import pallas as pl
from jax.experimental.pallas import tpu as pltpu
from jax.sharding import PartitionSpec as P

LANES = 128
ACROSS = 256
PIECE = 2048
ORDER = (2, 1, 3, 0)
GROUPS = 4
ROWS = PIECE // ACROSS
SLICES = 4
VMEM_GRANT = 52 * 1024 * 1024 + 512 * 1024

f32 = jnp.float32
bf16 = jnp.bfloat16


def make_tables(half_rows):
    total = 2 * half_rows * ACROSS
    freq = np.arange(half_rows)[:, None]
    row = np.arange(half_rows)[None, :]
    across = np.arange(ACROSS)
    angle = (row * (2 * freq + 1)) % (4 * half_rows) * (2 * math.pi / (4 * half_rows))
    chunk = half_rows // 2
    cos, sin = np.cos(angle), np.sin(angle)
    first = np.concatenate([cos[:chunk], -sin[:chunk], cos[chunk:], -sin[chunk:]], 0)
    last = np.concatenate([cos, -sin], 0).T
    twist = across[None, :] * (2 * freq + 1) * (2 * math.pi / (2 * total))
    inner = (across[:, None] * across[None, :]) % ACROSS * (2 * math.pi / ACROSS)
    re, im = np.cos(inner), -np.sin(inner)
    second = np.block([[re, im], [-im, re]])
    back = np.block([[re, -im], [im, re]])
    narrow = [t.astype(np.float32).astype(bf16) for t in (first, last, second, back)]
    return narrow + [np.cos(twist).astype(np.float32), -np.sin(twist).astype(np.float32)]


def kernel(
    parts,
    q_hbm, k_hbm, v_hbm, go_hbm, h_hbm,
    first_hbm, last_hbm, second_hbm, back_hbm, tre_hbm, tim_hbm,
    gq_ref, gk_ref, gv_ref, gf0_ref, gf1_ref,
    q_ref, k_ref, v_ref, go_ref, h_ref,
    first_ref, last_ref, second_ref, back_ref, tre_ref, tim_ref,
    turn_ref, msg_x, msg_g, msg_c, msg_m, got_x, got_g, got_c, got_m,
    signal_ref, mid_ref, spec_h, spec_x, spec_g,
    lag_ref, lag_in, pair_ref, pair_in, total_ref,
    window_sem, load_sem, send_sem, recv_sem, pair_send, pair_recv,
    high_send, high_recv, share_send, share_recv,
):
    half_rows = parts * ROWS
    seq = half_rows * ACROSS
    me = lax.axis_index("ctx")
    group = lax.axis_index("dp")
    core = lax.rem(group, 2)
    high = group // 2
    other_core = high * 2 + (1 - core)
    other_high = (1 - high) * 2 + core
    MESH = pl.DeviceIdType.MESH

    size = parts // GROUPS
    plane, spot = me // size, lax.rem(me, size)

    def sent_rows(i):
        return pl.multiple_of(lax.rem(plane + ORDER[i], GROUPS) * size, size)

    def got_rows(i):
        return pl.multiple_of(lax.rem(plane + GROUPS - ORDER[i], GROUPS) * size, size)

    barrier = pltpu.get_barrier_semaphore()

    def greet(step, carry):
        pl.semaphore_signal(
            barrier, inc=1, device_id=(lax.rem(me + step, parts), group), device_id_type=MESH
        )
        return carry

    lax.fori_loop(1, parts, greet, 0)
    pl.semaphore_signal(barrier, inc=1, device_id=(me, other_core), device_id_type=MESH)
    pl.semaphore_signal(barrier, inc=1, device_id=(me, other_high), device_id_type=MESH)

    windows = ((k_hbm, k_ref), (v_hbm, v_ref), (go_hbm, go_ref), (q_hbm, q_ref))
    window_loads = []
    for pair in (windows[:2], windows[2:]):
        for i in range(GROUPS):
            for src, dst in pair:
                rows = pl.ds(sent_rows(i), size)
                load = pltpu.make_async_copy(
                    src.at[rows], dst.at[rows], window_sem.at[len(window_loads)]
                )
                load.start()
                window_loads.append(load)
    loads = [
        pltpu.make_async_copy(src, dst, load_sem.at[i])
        for i, (src, dst) in enumerate(
            (
                (h_hbm, h_ref),
                (first_hbm, first_ref),
                (tre_hbm, tre_ref),
                (tim_hbm, tim_ref),
                (second_hbm, second_ref),
                (back_hbm, back_ref),
                (last_hbm, last_ref),
            )
        )
    ]
    for load in loads:
        load.start()

    def gate(a_ref, b_ref, msg_ref, i):
        start = sent_rows(i)
        rows = pl.ds(start, size)
        for j in range(PIECE // LANES):
            cols = slice(j * LANES, (j + 1) * LANES)
            slot = (j % 2) * ROWS + j // 2
            turn_ref[pl.ds(slot, size, stride=16), :] = a_ref[rows, cols].astype(f32) * b_ref[
                rows, cols
            ].astype(f32)
        msg_ref[rows] = turn_ref[...].reshape(size, 16, LANES).astype(bf16)

    def send_group(msg_ref, got_ref, which, i):
        start = sent_rows(i)

        def send(step, carry):
            to = start + lax.rem(spot + step, size)
            pltpu.make_async_remote_copy(
                src_ref=msg_ref.at[to],
                dst_ref=got_ref.at[me],
                send_sem=send_sem.at[which],
                recv_sem=recv_sem.at[which, i],
                device_id=(to, group),
                device_id_type=MESH,
            ).start()
            return carry

        lax.fori_loop(1 if ORDER[i] == 0 else 0, size, send, 0)
        if ORDER[i] == 0:
            got_ref[me] = msg_ref[me]

    def wait_group(got_ref, which, i):
        count = size - 1 if ORDER[i] == 0 else size
        if count:
            some = got_ref.at[pl.ds(0, count)]
            pltpu.make_async_copy(some, some, recv_sem.at[which, i]).wait()

    def wait_all(got_ref, which):
        for i in range(GROUPS):
            wait_group(got_ref, which, i)

    def unfold(got_ref):
        got = got_ref[...].astype(f32)
        for half in range(2):
            signal_ref[:, half * LANES : (half + 1) * LANES] = (
                got[:, half * ROWS : (half + 1) * ROWS, :].reshape(half_rows, LANES).astype(bf16)
            )

    chunk = half_rows // 2

    def forward(spec_ref):
        def body(c, carry):
            rows = pl.ds(pl.multiple_of(c * chunk, chunk), chunk)
            both = jnp.dot(
                first_ref[pl.ds(pl.multiple_of(c * 2 * chunk, 2 * chunk), 2 * chunk), :],
                signal_ref[...],
                preferred_element_type=f32,
            )
            re, im = both[:chunk], both[chunk:]
            tre, tim = tre_ref[rows, :], tim_ref[rows, :]
            turned = jnp.concatenate([re * tre - im * tim, re * tim + im * tre], 1).astype(bf16)
            spec_ref[rows, :] = jnp.dot(turned, second_ref[...], preferred_element_type=f32)
            return carry

        lax.fori_loop(0, 2, body, 0)

    def inverse_mid(a_spec, b_spec, conj):
        def body(c, carry):
            rows = pl.ds(pl.multiple_of(c * chunk, chunk), chunk)
            a_re, a_im = a_spec[rows, :ACROSS], a_spec[rows, ACROSS:]
            b_re, b_im = b_spec[rows, :ACROSS], b_spec[rows, ACROSS:]
            if conj:
                re, im = a_re * b_re + a_im * b_im, a_re * b_im - a_im * b_re
            else:
                re, im = a_re * b_re - a_im * b_im, a_re * b_im + a_im * b_re
            inner = jnp.dot(
                jnp.concatenate([re, im], 1).astype(bf16), back_ref[...], preferred_element_type=f32
            )
            re, im = inner[:, :ACROSS], inner[:, ACROSS:]
            tre, tim = tre_ref[rows, :], tim_ref[rows, :]
            mid_ref[rows, :] = (re * tre + im * tim).astype(bf16)
            mid_ref[pl.ds(pl.multiple_of(half_rows + c * chunk, chunk), chunk), :] = (
                im * tre - re * tim
            ).astype(bf16)
            return carry

        lax.fori_loop(0, 2, body, 0)

    def inverse_rows_and_send(msg_ref, got_ref, which):
        for i in range(GROUPS):
            start = sent_rows(i)
            rows = pl.ds(pl.multiple_of(start * ROWS, size * ROWS), size * ROWS)
            out = jnp.dot(last_ref[rows, :], mid_ref[...], preferred_element_type=f32) * (1.0 / seq)
            out = jnp.concatenate(
                [
                    out[:, :LANES].reshape(size, ROWS, LANES),
                    out[:, LANES:].reshape(size, ROWS, LANES),
                ],
                1,
            )
            msg_ref[pl.ds(start, size)] = out.astype(bf16)
            send_group(msg_ref, got_ref, which, i)

    for i in range(GROUPS):
        window_loads[2 * i].wait()
        window_loads[2 * i + 1].wait()
        gate(k_ref, v_ref, msg_x, i)
        if i == 0:
            pl.semaphore_wait(barrier, parts + 1)
        send_group(msg_x, got_x, 0, i)
    for i in range(GROUPS):
        window_loads[2 * (GROUPS + i)].wait()
        window_loads[2 * (GROUPS + i) + 1].wait()
        gate(go_ref, q_ref, msg_g, i)
        send_group(msg_g, got_g, 1, i)

    root = math.sqrt(seq)
    loads[0].wait()
    for half in range(2):
        signal_ref[:, half * LANES : (half + 1) * LANES] = (
            h_ref[pl.ds(half, half_rows, stride=2), :] * (1.0 / root)
        ).astype(bf16)
    for load in loads[1:5]:
        load.wait()
    forward(spec_h)

    wait_all(got_x, 0)
    unfold(got_x)
    forward(spec_x)
    for load in loads[5:]:
        load.wait()
    inverse_mid(spec_h, spec_x, False)
    inverse_rows_and_send(msg_c, got_c, 2)

    wait_all(got_g, 1)
    unfold(got_g)
    forward(spec_g)

    inverse_mid(spec_h, spec_g, True)
    inverse_rows_and_send(msg_m, got_m, 3)
    inverse_mid(spec_x, spec_g, True)

    def lag_half(c):
        rows = pl.ds(pl.multiple_of(c * chunk, chunk), chunk)
        lag_ref[c] = (
            jnp.dot(last_ref[rows, :], mid_ref[...], preferred_element_type=f32)
            * (1.0 / (seq * root))
        ).astype(bf16)

    lag_half(1 - core)
    to_core = pltpu.make_async_remote_copy(
        src_ref=lag_ref.at[1 - core],
        dst_ref=lag_in,
        send_sem=pair_send.at[0],
        recv_sem=pair_recv.at[0],
        device_id=(me, other_core),
        device_id_type=MESH,
    )
    to_core.start()
    lag_half(core)

    to_core.wait_recv()
    quarter = half_rows // 8
    to_high = [
        pltpu.make_async_remote_copy(
            src_ref=pair_ref.at[pl.ds(n * quarter, quarter)],
            dst_ref=pair_in.at[pl.ds(n * quarter, quarter)],
            send_sem=high_send.at[n],
            recv_sem=high_recv.at[n],
            device_id=(me, other_high),
            device_id_type=MESH,
        )
        for n in range(4)
    ]
    for n in range(4):
        rows = pl.ds(n * quarter, quarter)
        pair_ref[rows] = (lag_ref[core, rows].astype(f32) + lag_in[rows].astype(f32)).astype(bf16)
        to_high[n].start()

    def finish(got_ref, which, i, terms):
        wait_group(got_ref, which, i)
        rows = pl.ds(got_rows(i), size)
        turn_ref[...] = got_ref[rows].astype(f32).reshape(size * 16, LANES)
        for j in range(PIECE // LANES):
            cols = slice(j * LANES, (j + 1) * LANES)
            slot = (j % 2) * ROWS + j // 2
            value = turn_ref[pl.ds(slot, size, stride=16), :]
            for factor_ref, out_ref in terms:
                out_ref[rows, cols] = (factor_ref[rows, cols].astype(f32) * value).astype(bf16)

    for i in range(GROUPS):
        finish(got_c, 2, i, ((go_ref, gq_ref),))

    for i in (0, 1, 2, 3):
        finish(got_m, 3, i, ((v_ref, gk_ref), (k_ref, gv_ref)))

    to_core_again = []
    for n in range(4):
        rows = pl.ds(n * quarter, quarter)
        to_high[n].wait_recv()
        total_ref[core, rows] = pair_ref[rows].astype(f32) + pair_in[rows].astype(f32)
        copy = pltpu.make_async_remote_copy(
            src_ref=total_ref.at[core, rows],
            dst_ref=total_ref.at[core, rows],
            send_sem=share_send.at[n],
            recv_sem=share_recv.at[n],
            device_id=(me, other_core),
            device_id_type=MESH,
        )
        copy.start()
        to_core_again.append(copy)
    for copy in to_core_again:
        copy.wait_recv()
    for c, gf_ref in enumerate((gf0_ref, gf1_ref)):
        for half in range(2):
            gf_ref[pl.ds(half, chunk, stride=2), :] = total_ref[
                c, :, half * LANES : (half + 1) * LANES
            ]

    for which, ref in enumerate((msg_x, msg_g, msg_c, msg_m)):
        some = ref.at[pl.ds(0, parts - 1)]
        pltpu.make_async_copy(some, some, send_sem.at[which]).wait()
    to_core.wait_send()
    for copy in to_high + to_core_again:
        copy.wait_send()


def write_out(*refs):
    sources, targets, sem = refs[:5], refs[5:9], refs[9]
    copies = []
    for i, source in enumerate(sources):
        height = source.shape[0]
        step = height // SLICES
        target, base = (targets[i], 0) if i < 3 else (targets[3], (i - 3) * height)
        for part in range(SLICES):
            copies.append(
                pltpu.make_async_copy(
                    source.at[pl.ds(part * step, step)],
                    target.at[pl.ds(base + part * step, step)],
                    sem.at[len(copies)],
                )
            )
    for copy in copies:
        copy.start()
    for copy in copies:
        copy.wait()


def per_device(parts, query_in, key_in, value_in, grad_out, filter_raw):
    half_rows = parts * ROWS
    seq = half_rows * ACROSS
    tables = make_tables(half_rows)
    vmem = pl.BlockSpec(memory_space=pltpu.VMEM)
    hbm = pl.BlockSpec(memory_space=pltpu.HBM)
    window = jax.ShapeDtypeStruct((parts, PIECE), bf16)
    taps = jax.ShapeDtypeStruct((seq // (2 * LANES), LANES), f32)
    message = pltpu.VMEM((parts, 16, LANES), bf16)
    spectrum = pltpu.VMEM((half_rows, 2 * ACROSS), f32)
    half = (half_rows // 2, ACROSS)
    outs = pl.pallas_call(
        functools.partial(kernel, parts),
        out_shape=(window, window, window, taps, taps),
        in_specs=[hbm] * 11,
        out_specs=(vmem,) * 5,
        scratch_shapes=[pltpu.VMEM((parts, PIECE), bf16)] * 4
        + [pltpu.VMEM((seq // LANES, LANES), f32)]
        + [pltpu.VMEM(t.shape, t.dtype) for t in tables]
        + [pltpu.VMEM((parts // GROUPS * 16, LANES), f32)]
        + [message] * 8
        + [
            pltpu.VMEM((half_rows, ACROSS), bf16),
            pltpu.VMEM((2 * half_rows, ACROSS), bf16),
            spectrum,
            spectrum,
            spectrum,
            pltpu.VMEM((2,) + half, bf16),
            pltpu.VMEM(half, bf16),
            pltpu.VMEM(half, bf16),
            pltpu.VMEM(half, bf16),
            pltpu.VMEM((2,) + half, f32),
            pltpu.SemaphoreType.DMA((4 * GROUPS,)),
            pltpu.SemaphoreType.DMA((7,)),
            pltpu.SemaphoreType.DMA((4,)),
            pltpu.SemaphoreType.DMA((4, GROUPS)),
            pltpu.SemaphoreType.DMA((1,)),
            pltpu.SemaphoreType.DMA((1,)),
            pltpu.SemaphoreType.DMA((4,)),
            pltpu.SemaphoreType.DMA((4,)),
            pltpu.SemaphoreType.DMA((4,)),
            pltpu.SemaphoreType.DMA((4,)),
        ],
        compiler_params=pltpu.CompilerParams(
            collective_id=0, has_side_effects=True, vmem_limit_bytes=VMEM_GRANT
        ),
        name="gated_conv_backward",
    )(
        query_in,
        key_in,
        value_in,
        grad_out,
        filter_raw.reshape(seq // LANES, LANES),
        *(jnp.asarray(t) for t in tables),
    )
    outs = pl.pallas_call(
        write_out,
        out_shape=(window, window, window, jax.ShapeDtypeStruct((seq // LANES, LANES), f32)),
        in_specs=[pl.BlockSpec(memory_space=pl.ANY)] * 5,
        out_specs=[hbm] * 4,
        scratch_shapes=[pltpu.SemaphoreType.DMA((5 * SLICES,))],
        compiler_params=pltpu.CompilerParams(vmem_limit_bytes=VMEM_GRANT),
        name="write_out",
    )(*outs)
    return (outs[0], outs[1], outs[2], outs[3].reshape(1, seq))


def solution(mesh):
    return jax.shard_map(
        functools.partial(per_device, mesh.shape["ctx"]),
        mesh=mesh,
        in_specs=(P("dp", "ctx"), P("dp", "ctx"), P("dp", "ctx"), P("dp", "ctx"), P("ctx", None)),
        out_specs=(P("dp", "ctx"), P("dp", "ctx"), P("dp", "ctx"), P("ctx", None)),
        check_vma=False,
    )
```

```python
import functools
import math

import jax
import jax.numpy as jnp
import numpy as np
from jax import lax
from jax.experimental import pallas as pl
from jax.experimental.pallas import tpu as pltpu
from jax.sharding import PartitionSpec as P

LANES = 128
ACROSS = 256
PIECE = 2048
ORDER = (2, 1, 3, 0)
GROUPS = 4
ROWS = PIECE // ACROSS
SLICES = 4
VMEM_GRANT = 52 * 1024 * 1024 + 512 * 1024

f32 = jnp.float32
bf16 = jnp.bfloat16


def make_tables(half_rows):
    total = 2 * half_rows * ACROSS
    freq = np.arange(half_rows)[:, None]
    row = np.arange(half_rows)[None, :]
    across = np.arange(ACROSS)
    angle = (row * (2 * freq + 1)) % (4 * half_rows) * (2 * math.pi / (4 * half_rows))
    chunk = half_rows // 2
    cos, sin = np.cos(angle), np.sin(angle)
    first = np.concatenate([cos[:chunk], -sin[:chunk], cos[chunk:], -sin[chunk:]], 0)
    last = np.concatenate([cos, -sin], 0).T
    twist = across[None, :] * (2 * freq + 1) * (2 * math.pi / (2 * total))
    inner = (across[:, None] * across[None, :]) % ACROSS * (2 * math.pi / ACROSS)
    re, im = np.cos(inner), -np.sin(inner)
    second = np.block([[re, im], [-im, re]])
    back = np.block([[re, -im], [im, re]])
    narrow = [t.astype(np.float32).astype(bf16) for t in (first, last, second, back)]
    return narrow + [np.cos(twist).astype(np.float32), -np.sin(twist).astype(np.float32)]


def kernel(
    parts,
    q_hbm, k_hbm, v_hbm, go_hbm, h_hbm,
    first_hbm, last_hbm, second_hbm, back_hbm, tre_hbm, tim_hbm,
    gq_ref, gk_ref, gv_ref, gf0_ref, gf1_ref,
    q_ref, k_ref, v_ref, go_ref, h_ref,
    first_ref, last_ref, second_ref, back_ref, tre_ref, tim_ref,
    turn_ref, msg_x, msg_g, msg_c, msg_m, got_x, got_g, got_c, got_m,
    signal_ref, mid_ref, spec_h, spec_x, spec_g,
    lag_ref, lag_in, pair_ref, pair_in, total_ref,
    window_sem, load_sem, send_sem, recv_sem, pair_send, pair_recv,
    high_send, high_recv, share_send, share_recv,
):
    half_rows = parts * ROWS
    seq = half_rows * ACROSS
    me = lax.axis_index("ctx")
    group = lax.axis_index("dp")
    core = lax.rem(group, 2)
    high = group // 2
    other_core = high * 2 + (1 - core)
    other_high = (1 - high) * 2 + core
    MESH = pl.DeviceIdType.MESH

    size = parts // GROUPS
    plane, spot = me // size, lax.rem(me, size)

    odd = lax.rem(spot, 2)

    def distance(i):
        return (2, 1 + 2 * odd, 3 - 2 * odd, 0)[i]

    def sent_rows(i):
        return pl.multiple_of(lax.rem(plane + distance(i), GROUPS) * size, size)

    def got_rows(i):
        return pl.multiple_of(lax.rem(plane + GROUPS - ORDER[i], GROUPS) * size, size)

    barrier = pltpu.get_barrier_semaphore()

    def greet(step, carry):
        pl.semaphore_signal(
            barrier, inc=1, device_id=(lax.rem(me + step, parts), group), device_id_type=MESH
        )
        return carry

    lax.fori_loop(1, parts, greet, 0)
    pl.semaphore_signal(barrier, inc=1, device_id=(me, other_core), device_id_type=MESH)
    pl.semaphore_signal(barrier, inc=1, device_id=(me, other_high), device_id_type=MESH)

    windows = ((k_hbm, k_ref), (v_hbm, v_ref), (go_hbm, go_ref), (q_hbm, q_ref))
    window_loads = []
    for pair in (windows[:2], windows[2:]):
        for i in range(GROUPS):
            for src, dst in pair:
                rows = pl.ds(sent_rows(i), size)
                load = pltpu.make_async_copy(
                    src.at[rows], dst.at[rows], window_sem.at[len(window_loads)]
                )
                load.start()
                window_loads.append(load)
    loads = [
        pltpu.make_async_copy(src, dst, load_sem.at[i])
        for i, (src, dst) in enumerate(
            (
                (h_hbm, h_ref),
                (first_hbm, first_ref),
                (tre_hbm, tre_ref),
                (tim_hbm, tim_ref),
                (second_hbm, second_ref),
                (back_hbm, back_ref),
                (last_hbm, last_ref),
            )
        )
    ]
    for load in loads:
        load.start()

    def gate(a_ref, b_ref, msg_ref, i):
        start = sent_rows(i)
        rows = pl.ds(start, size)
        for j in range(PIECE // LANES):
            cols = slice(j * LANES, (j + 1) * LANES)
            slot = (j % 2) * ROWS + j // 2
            turn_ref[pl.ds(slot, size, stride=16), :] = a_ref[rows, cols].astype(f32) * b_ref[
                rows, cols
            ].astype(f32)
        msg_ref[rows] = turn_ref[...].reshape(size, 16, LANES).astype(bf16)

    def send_group(msg_ref, got_ref, which, i):
        start = sent_rows(i)

        def send(step, carry):
            to = start + lax.rem(spot + step, size)
            pltpu.make_async_remote_copy(
                src_ref=msg_ref.at[to],
                dst_ref=got_ref.at[me],
                send_sem=send_sem.at[which],
                recv_sem=recv_sem.at[which, distance(i)],
                device_id=(to, group),
                device_id_type=MESH,
            ).start()
            return carry

        lax.fori_loop(1 if ORDER[i] == 0 else 0, size, send, 0)
        if ORDER[i] == 0:
            got_ref[me] = msg_ref[me]

    def wait_group(got_ref, which, i):
        count = size - 1 if ORDER[i] == 0 else size
        if count:
            some = got_ref.at[pl.ds(0, count)]
            pltpu.make_async_copy(some, some, recv_sem.at[which, ORDER[i]]).wait()

    def wait_all(got_ref, which):
        for i in range(GROUPS):
            wait_group(got_ref, which, i)

    def unfold(got_ref):
        got = got_ref[...].astype(f32)
        for half in range(2):
            signal_ref[:, half * LANES : (half + 1) * LANES] = (
                got[:, half * ROWS : (half + 1) * ROWS, :].reshape(half_rows, LANES).astype(bf16)
            )

    chunk = half_rows // 2

    def forward(spec_ref):
        def body(c, carry):
            rows = pl.ds(pl.multiple_of(c * chunk, chunk), chunk)
            both = jnp.dot(
                first_ref[pl.ds(pl.multiple_of(c * 2 * chunk, 2 * chunk), 2 * chunk), :],
                signal_ref[...],
                preferred_element_type=f32,
            )
            re, im = both[:chunk], both[chunk:]
            tre, tim = tre_ref[rows, :], tim_ref[rows, :]
            turned = jnp.concatenate([re * tre - im * tim, re * tim + im * tre], 1).astype(bf16)
            spec_ref[rows, :] = jnp.dot(turned, second_ref[...], preferred_element_type=f32)
            return carry

        lax.fori_loop(0, 2, body, 0)

    def inverse_mid(a_spec, b_spec, conj):
        def body(c, carry):
            rows = pl.ds(pl.multiple_of(c * chunk, chunk), chunk)
            a_re, a_im = a_spec[rows, :ACROSS], a_spec[rows, ACROSS:]
            b_re, b_im = b_spec[rows, :ACROSS], b_spec[rows, ACROSS:]
            if conj:
                re, im = a_re * b_re + a_im * b_im, a_re * b_im - a_im * b_re
            else:
                re, im = a_re * b_re - a_im * b_im, a_re * b_im + a_im * b_re
            inner = jnp.dot(
                jnp.concatenate([re, im], 1).astype(bf16), back_ref[...], preferred_element_type=f32
            )
            re, im = inner[:, :ACROSS], inner[:, ACROSS:]
            tre, tim = tre_ref[rows, :], tim_ref[rows, :]
            mid_ref[rows, :] = (re * tre + im * tim).astype(bf16)
            mid_ref[pl.ds(pl.multiple_of(half_rows + c * chunk, chunk), chunk), :] = (
                im * tre - re * tim
            ).astype(bf16)
            return carry

        lax.fori_loop(0, 2, body, 0)

    def inverse_rows_and_send(msg_ref, got_ref, which):
        for i in range(GROUPS):
            start = sent_rows(i)
            rows = pl.ds(pl.multiple_of(start * ROWS, size * ROWS), size * ROWS)
            out = jnp.dot(last_ref[rows, :], mid_ref[...], preferred_element_type=f32) * (1.0 / seq)
            out = jnp.concatenate(
                [
                    out[:, :LANES].reshape(size, ROWS, LANES),
                    out[:, LANES:].reshape(size, ROWS, LANES),
                ],
                1,
            )
            msg_ref[pl.ds(start, size)] = out.astype(bf16)
            send_group(msg_ref, got_ref, which, i)

    for i in range(GROUPS):
        window_loads[2 * i].wait()
        window_loads[2 * i + 1].wait()
        gate(k_ref, v_ref, msg_x, i)
        if i == 0:
            pl.semaphore_wait(barrier, parts + 1)
        send_group(msg_x, got_x, 0, i)
    for i in range(GROUPS):
        window_loads[2 * (GROUPS + i)].wait()
        window_loads[2 * (GROUPS + i) + 1].wait()
        gate(go_ref, q_ref, msg_g, i)
        send_group(msg_g, got_g, 1, i)

    root = math.sqrt(seq)
    loads[0].wait()
    for half in range(2):
        signal_ref[:, half * LANES : (half + 1) * LANES] = (
            h_ref[pl.ds(half, half_rows, stride=2), :] * (1.0 / root)
        ).astype(bf16)
    for load in loads[1:5]:
        load.wait()
    forward(spec_h)

    wait_all(got_x, 0)
    unfold(got_x)
    forward(spec_x)
    for load in loads[5:]:
        load.wait()
    inverse_mid(spec_h, spec_x, False)
    inverse_rows_and_send(msg_c, got_c, 2)

    wait_all(got_g, 1)
    unfold(got_g)
    forward(spec_g)

    inverse_mid(spec_h, spec_g, True)
    inverse_rows_and_send(msg_m, got_m, 3)
    inverse_mid(spec_x, spec_g, True)

    def lag_body(c, carry):
        rows = pl.ds(pl.multiple_of(c * chunk, chunk), chunk)
        lag_ref[c] = (
            jnp.dot(last_ref[rows, :], mid_ref[...], preferred_element_type=f32)
            * (1.0 / (seq * root))
        ).astype(bf16)
        return carry

    lax.fori_loop(0, 2, lag_body, 0)

    to_core = pltpu.make_async_remote_copy(
        src_ref=lag_ref.at[1 - core],
        dst_ref=lag_in,
        send_sem=pair_send.at[0],
        recv_sem=pair_recv.at[0],
        device_id=(me, other_core),
        device_id_type=MESH,
    )
    to_core.start()

    to_core.wait_recv()
    pair_ref[...] = (lag_ref[core].astype(f32) + lag_in[...].astype(f32)).astype(bf16)
    quarter = half_rows // 8
    to_high = [
        pltpu.make_async_remote_copy(
            src_ref=pair_ref.at[pl.ds(n * quarter, quarter)],
            dst_ref=pair_in.at[pl.ds(n * quarter, quarter)],
            send_sem=high_send.at[n],
            recv_sem=high_recv.at[n],
            device_id=(me, other_high),
            device_id_type=MESH,
        )
        for n in range(4)
    ]
    for copy in to_high:
        copy.start()

    def finish(got_ref, which, i, terms):
        wait_group(got_ref, which, i)
        rows = pl.ds(got_rows(i), size)
        turn_ref[...] = got_ref[rows].astype(f32).reshape(size * 16, LANES)
        for j in range(PIECE // LANES):
            cols = slice(j * LANES, (j + 1) * LANES)
            slot = (j % 2) * ROWS + j // 2
            value = turn_ref[pl.ds(slot, size, stride=16), :]
            for factor_ref, out_ref in terms:
                out_ref[rows, cols] = (factor_ref[rows, cols].astype(f32) * value).astype(bf16)

    for i in range(GROUPS):
        finish(got_c, 2, i, ((go_ref, gq_ref),))

    for i in (0, 1, 2, 3):
        finish(got_m, 3, i, ((v_ref, gk_ref), (k_ref, gv_ref)))

    to_core_again = []
    for n in range(4):
        rows = pl.ds(n * quarter, quarter)
        to_high[n].wait_recv()
        total_ref[core, rows] = pair_ref[rows].astype(f32) + pair_in[rows].astype(f32)
        copy = pltpu.make_async_remote_copy(
            src_ref=total_ref.at[core, rows],
            dst_ref=total_ref.at[core, rows],
            send_sem=share_send.at[n],
            recv_sem=share_recv.at[n],
            device_id=(me, other_core),
            device_id_type=MESH,
        )
        copy.start()
        to_core_again.append(copy)
    for copy in to_core_again:
        copy.wait_recv()
    for c, gf_ref in enumerate((gf0_ref, gf1_ref)):
        for half in range(2):
            gf_ref[pl.ds(half, chunk, stride=2), :] = total_ref[
                c, :, half * LANES : (half + 1) * LANES
            ]

    for which, ref in enumerate((msg_x, msg_g, msg_c, msg_m)):
        some = ref.at[pl.ds(0, parts - 1)]
        pltpu.make_async_copy(some, some, send_sem.at[which]).wait()
    to_core.wait_send()
    for copy in to_high + to_core_again:
        copy.wait_send()


def write_out(*refs):
    sources, targets, sem = refs[:5], refs[5:9], refs[9]
    copies = []
    for i, source in enumerate(sources):
        height = source.shape[0]
        step = height // SLICES
        target, base = (targets[i], 0) if i < 3 else (targets[3], (i - 3) * height)
        for part in range(SLICES):
            copies.append(
                pltpu.make_async_copy(
                    source.at[pl.ds(part * step, step)],
                    target.at[pl.ds(base + part * step, step)],
                    sem.at[len(copies)],
                )
            )
    for copy in copies:
        copy.start()
    for copy in copies:
        copy.wait()


def per_device(parts, query_in, key_in, value_in, grad_out, filter_raw):
    half_rows = parts * ROWS
    seq = half_rows * ACROSS
    tables = make_tables(half_rows)
    vmem = pl.BlockSpec(memory_space=pltpu.VMEM)
    hbm = pl.BlockSpec(memory_space=pltpu.HBM)
    window = jax.ShapeDtypeStruct((parts, PIECE), bf16)
    taps = jax.ShapeDtypeStruct((seq // (2 * LANES), LANES), f32)
    message = pltpu.VMEM((parts, 16, LANES), bf16)
    spectrum = pltpu.VMEM((half_rows, 2 * ACROSS), f32)
    half = (half_rows // 2, ACROSS)
    outs = pl.pallas_call(
        functools.partial(kernel, parts),
        out_shape=(window, window, window, taps, taps),
        in_specs=[hbm] * 11,
        out_specs=(vmem,) * 5,
        scratch_shapes=[pltpu.VMEM((parts, PIECE), bf16)] * 4
        + [pltpu.VMEM((seq // LANES, LANES), f32)]
        + [pltpu.VMEM(t.shape, t.dtype) for t in tables]
        + [pltpu.VMEM((parts // GROUPS * 16, LANES), f32)]
        + [message] * 8
        + [
            pltpu.VMEM((half_rows, ACROSS), bf16),
            pltpu.VMEM((2 * half_rows, ACROSS), bf16),
            spectrum,
            spectrum,
            spectrum,
            pltpu.VMEM((2,) + half, bf16),
            pltpu.VMEM(half, bf16),
            pltpu.VMEM(half, bf16),
            pltpu.VMEM(half, bf16),
            pltpu.VMEM((2,) + half, f32),
            pltpu.SemaphoreType.DMA((4 * GROUPS,)),
            pltpu.SemaphoreType.DMA((7,)),
            pltpu.SemaphoreType.DMA((4,)),
            pltpu.SemaphoreType.DMA((4, GROUPS)),
            pltpu.SemaphoreType.DMA((1,)),
            pltpu.SemaphoreType.DMA((1,)),
            pltpu.SemaphoreType.DMA((4,)),
            pltpu.SemaphoreType.DMA((4,)),
            pltpu.SemaphoreType.DMA((4,)),
            pltpu.SemaphoreType.DMA((4,)),
        ],
        compiler_params=pltpu.CompilerParams(
            collective_id=0, has_side_effects=True, vmem_limit_bytes=VMEM_GRANT
        ),
        name="gated_conv_backward",
    )(
        query_in,
        key_in,
        value_in,
        grad_out,
        filter_raw.reshape(seq // LANES, LANES),
        *(jnp.asarray(t) for t in tables),
    )
    outs = pl.pallas_call(
        write_out,
        out_shape=(window, window, window, jax.ShapeDtypeStruct((seq // LANES, LANES), f32)),
        in_specs=[pl.BlockSpec(memory_space=pl.ANY)] * 5,
        out_specs=[hbm] * 4,
        scratch_shapes=[pltpu.SemaphoreType.DMA((5 * SLICES,))],
        compiler_params=pltpu.CompilerParams(vmem_limit_bytes=VMEM_GRANT),
        name="write_out",
    )(*outs)
    return (outs[0], outs[1], outs[2], outs[3].reshape(1, seq))


def solution(mesh):
    return jax.shard_map(
        functools.partial(per_device, mesh.shape["ctx"]),
        mesh=mesh,
        in_specs=(P("dp", "ctx"), P("dp", "ctx"), P("dp", "ctx"), P("dp", "ctx"), P("ctx", None)),
        out_specs=(P("dp", "ctx"), P("dp", "ctx"), P("dp", "ctx"), P("ctx", None)),
        check_vma=False,
    )
```
